32 devices in a mesh: feat: 2 (over y), rows: 16 (over z, x, core).
Axes of the slice: x: 2, y: 2, z: 4, core: 2. Of those that a mesh axis runs over, the one named last changes fastest.
Arguments:
- features: bfloat16 [4096, 2048], P('rows', 'feat'), may hold values from -6 to 6
- labels: int32 [4096], P('rows'), may hold values from 0 to 639
- inv_gram: float32 [2, 1024, 1024], P('feat'), may hold values from -1 to 1, as said below
Outputs:
- weights: float32 [2048, 640], P(('feat', 'rows'))
- after_block: float32 [2, 4096, 640], P('feat', 'rows')
The draws below stay inside these ranges and needn't reach their ends.
Inputs may be any that keep to these rules, and one draw needn't show every extreme that they name: Each of the 2 matrices of inv_gram is symmetric.
All inputs are finite; a program needn't handle non-finite values.
Results may differ from the reference program's by a relative error of at most 0.0094.
Values sent between devices are 32-bit elements; how exact they have to be, the bound alone decides.
A program may use at most 64 MiB of HBM per device.

```python
import math
import jax
import jax.numpy as jnp
from jax import lax

BW = 1024
C = 640
ROW_DEV = 256
NBLK = 2
ROWS = 4096


def draw_labels(key, part):
    keys = jax.random.split(jax.random.fold_in(key, 11), 4)
    half = C // 2
    narrow_span = max(half // 4, 1)
    shard_total = ROWS // ROW_DEV
    positions = jnp.arange(ROWS, dtype=jnp.int32)
    shard_ids = positions // ROW_DEV
    first_half = jax.random.randint(keys[0], (ROWS,), 0, 3 * shard_total) < shard_total + 2 * shard_ids
    narrow = jax.random.randint(keys[1], (ROWS,), 0, 2) == 0
    wide_ids = jax.random.randint(keys[2], (ROWS,), 0, half)
    narrow_ids = jax.random.randint(keys[3], (ROWS,), 0, narrow_span)
    within = jnp.where(narrow, narrow_ids, wide_ids)
    return jnp.where(first_half, within, half + within).astype(jnp.int32)


def draw_inv_gram(key, part):
    keys = jax.random.split(jax.random.fold_in(key, 23), 2)
    low_end, high_end = (0.5, 2.0)
    diag_values = jnp.exp(jax.random.uniform(keys[0], (NBLK, BW), jnp.float32, math.log(low_end), math.log(high_end)))
    noise = jax.random.normal(keys[1], (NBLK, BW, BW), jnp.float32) * (0.2 / math.sqrt(BW))
    symmetric = (noise + jnp.transpose(noise, (0, 2, 1))) / math.sqrt(2.0)
    identity = jnp.eye(BW, dtype=jnp.float32)
    return (0.25 / BW * (symmetric + diag_values[:, :, None] * identity[None, :, :])).astype(jnp.float32)


def strengthened(values, key, source, target, parts, factor):
    def block_of(axis_at):
        return (jnp.arange(values.shape[axis_at]) // (values.shape[axis_at] // parts)).reshape((-1,) + (1,) * (values.ndim - 1 - axis_at))

    one_side = jax.random.permutation(key, parts)[block_of(target)]
    second = (block_of(target) + parts // 2) % parts
    return jnp.where((block_of(source) == one_side) | (block_of(source) == second), factor * values, values)


def shard_levels(key, extent, cuts, low, top_value):
    loudness = 1.0
    for dim, blocks in cuts:
        heights = jax.random.uniform(jax.random.fold_in(jax.random.fold_in(key, 6), dim), (blocks,), jnp.float32, low / len(cuts), top_value / len(cuts))
        loudness = loudness * jnp.repeat(jnp.exp(heights), extent[dim] // blocks).reshape((-1,) + (1,) * (len(extent) - 1 - dim))
    return loudness


def noise_with(key, extent, scale, reach, pieces, heavy, kind=jnp.bfloat16):
    drawn = scale * jax.random.normal(key, extent, jnp.float32)
    if pieces:
        drawn = drawn * shard_levels(key, extent, pieces, -0.22, 0.18)
    return jnp.clip(strengthened(drawn, jax.random.fold_in(key, 3), *heavy), -reach, reach).astype(kind)


def setup_inputs(seed: int = 0) -> dict:
    arg_keys = jax.random.split(jax.random.key(seed), 4)
    features = noise_with(arg_keys[0], (ROWS, NBLK * BW), 1.0, 6.0, ((0, 16), (1, 2)), (0, 1, 16, 2.0))
    labels = draw_labels(jax.random.fold_in(arg_keys[3], 71), 0)
    inv_gram = draw_inv_gram(jax.random.fold_in(arg_keys[3], 71), 0)
    return {"features": features, "labels": labels, "inv_gram": inv_gram}


def reference(features, labels, inv_gram):
    total_rows = labels.shape[0]
    counts = jnp.zeros((C,), jnp.float32).at[labels].add(1.0)
    row_weight = total_rows / (C * counts[labels])
    class_ids = jnp.arange(C, dtype=jnp.int32)
    residual = (labels[:, None] == class_ids[None, :]).astype(jnp.float32)
    weight_list = []
    residual_list = []
    for index in range(NBLK):
        feature_block = features[:, index * BW:(index + 1) * BW]
        scaled = (row_weight[:, None] * residual).astype(jnp.bfloat16)
        partial_value = lax.dot_general(feature_block, scaled, (((0,), (0,)), ((), ())), preferred_element_type=jnp.float32)
        solved = jnp.dot(inv_gram[index], partial_value, precision=lax.Precision.HIGHEST, preferred_element_type=jnp.float32)
        residual = residual - jnp.dot(feature_block, solved.astype(jnp.bfloat16), preferred_element_type=jnp.float32)
        weight_list.append(solved)
        residual_list.append(residual)
    return jnp.concatenate(weight_list, axis=0), jnp.stack(residual_list, axis=0)
```

```python
import functools
import math

import jax
import jax.numpy as jnp
from jax import lax
from jax.experimental import pallas as pl
from jax.experimental.pallas import tpu as pltpu
from jax.sharding import PartitionSpec as P

C = 640
CHUNK = 128
CORES = 2
MESH = pl.DeviceIdType.MESH


def split(value):
    high = value.astype(jnp.bfloat16)
    return high, (value - high.astype(jnp.float32)).astype(jnp.bfloat16)


def kernel(
    groups, total_rows, order,
    x_ref, labels_ref, inv_ref, w_ref, out_ref,
    inv, xt, m_high, m_low, part, core_in, sum1, inner_in, sum2, outer_in, full, resid, after,
    row_weight, scale, cnt, cnt_core, cnt_inner, cnt_outer,
    inv_sem, cs, cr, xs, xr, zs, zr, zgs, zgr, xgs, xgr, cgs, cgr, ys, yr, ncs, ncr, nxs, nxr, nzs, nzr,
):
    n_feat, n_out, n_in = groups
    feat = lax.axis_index("feat")
    me = lax.axis_index("rows")
    core = lax.rem(me, CORES)
    inner = lax.rem(me // CORES, n_in)
    outer = me // (CORES * n_in)
    rows, width = x_ref.shape
    share = part.shape[-2]
    chunks = part.shape[0]

    def device(o, i, c):
        return (feat, (o * n_in + i) * CORES + c)

    sibling = device(outer, inner, 1 - core)

    def inner_at(d):
        return lax.rem(inner + d, n_in)

    def outer_at(d):
        return lax.rem(outer + d, n_out)

    def remote(src, dst, send, recv, where):
        return pltpu.make_async_remote_copy(
            src_ref=src, dst_ref=dst, send_sem=send, recv_sem=recv, device_id=where, device_id_type=MESH
        )

    inv_copy = pltpu.make_async_copy(inv_ref, inv, inv_sem)
    inv_copy.start()

    barrier = pltpu.get_barrier_semaphore()
    peers = [sibling]
    peers += [device(outer, inner_at(d), core) for d in range(1, n_in)]
    peers += [device(outer_at(d), inner, core) for d in range(1, n_out)]
    for peer in peers:
        pl.semaphore_signal(barrier, inc=1, device_id=peer, device_id_type=MESH)

    @pl.when(feat < n_feat - 1)
    def _():
        pl.semaphore_signal(barrier, inc=1, device_id=(feat + 1, me), device_id_type=MESH)

    @pl.when(feat > 0)
    def _():
        pl.semaphore_signal(barrier, inc=1, device_id=(feat - 1, me), device_id_type=MESH)

    labels = labels_ref[...]
    onehot = (labels == lax.broadcasted_iota(jnp.int32, (rows, C), 1)).astype(jnp.float32)
    cnt[0] = jnp.broadcast_to(jnp.sum(onehot, axis=0, keepdims=True), (8, C))

    @pl.when(feat == 0)
    def _():
        for k in range(chunks):
            resid[k] = onehot[:, k * CHUNK:(k + 1) * CHUNK]

    xt[...] = x_ref[...].T

    beside = (feat < n_feat - 1).astype(jnp.int32) + (feat > 0).astype(jnp.int32)
    pl.semaphore_wait(barrier, len(peers) + beside)

    n_core = remote(cnt.at[0], cnt_core, ncs, ncr, sibling)
    n_core.start()
    n_inner = [
        remote(cnt.at[1], cnt_inner.at[d - 1], nxs.at[d - 1], nxr.at[d - 1], device(outer, inner_at(d), core))
        for d in range(1, n_in)
    ]
    n_outer = [
        remote(cnt.at[2], cnt_outer.at[d - 1], nzs.at[d - 1], nzr.at[d - 1], device(outer_at(d), inner, core))
        for d in range(1, n_out)
    ]

    def count_core():
        n_core.wait_recv()
        cnt[1] = cnt[0] + cnt_core[...]
        for copy in n_inner:
            copy.start()

    def count_inner():
        total = cnt[1]
        for d, copy in enumerate(n_inner):
            copy.wait_recv()
            total = total + cnt_inner[d]
        cnt[2] = total
        for copy in n_outer:
            copy.start()

    def count_outer():
        total = cnt[2]
        for d, copy in enumerate(n_outer):
            copy.wait_recv()
            total = total + cnt_outer[d]
        return total

    def weights_of_classes():
        counts = count_outer()
        by_class = jnp.where(counts > 0, total_rows / (C * jnp.maximum(counts, 1.0)), 0.0)
        scale[...] = by_class.astype(jnp.bfloat16).astype(jnp.float32)

    def weights_of_rows():
        counts = count_outer()
        hot = (labels_ref[...] == lax.broadcasted_iota(jnp.int32, (rows, C), 1)).astype(jnp.float32)
        count_row = jnp.sum(hot * counts[0:1], axis=1, keepdims=True)
        row_weight[...] = total_rows / (C * count_row)
        scale[...] = jnp.ones_like(scale)

    def products():
        inv_copy.wait()
        block = min(256, width)

        @pl.loop(0, width // block)
        def _(j):
            columns = pl.ds(pl.multiple_of(j * block, block), block)
            high, low = split(inv[:, columns])
            x = x_ref[...]
            m = jnp.dot(x, high, preferred_element_type=jnp.float32)
            m = m + jnp.dot(x, low, preferred_element_type=jnp.float32)
            mh, ml = split(m)
            m_high[0:rows, columns] = mh
            m_low[0:rows, columns] = ml

        oh, ol = split(inv[pl.ds(pl.multiple_of(me * share, share), share), :])
        m_high[rows:rows + share, :] = oh
        m_low[rows:rows + share, :] = ol

    to_core, to_inner, to_outer, gather_outer, gather_inner, gather_core, to_next = [], [], [], [], [], [], []
    got_outer, got_inner, got_core = [], [], []
    for k in range(chunks):
        to_core.append(remote(part.at[k, :, :, 1 - core], core_in.at[k], cs.at[k], cr.at[k], sibling))
        to_inner.append([
            remote(sum1.at[k, :, inner_at(d)], inner_in.at[k, d - 1], xs.at[k, d - 1], xr.at[k, d - 1],
                   device(outer, inner_at(d), core))
            for d in range(1, n_in)
        ])
        to_outer.append([
            remote(sum2.at[k, outer_at(d)], outer_in.at[k, d - 1], zs.at[k, d - 1], zr.at[k, d - 1],
                   device(outer_at(d), inner, core))
            for d in range(1, n_out)
        ])
        own = full.at[k, outer, inner, core]
        gather_outer.append([
            remote(own, own, zgs.at[k, d - 1], zgr.at[k, d - 1], device(outer_at(d), inner, core))
            for d in range(1, n_out)
        ])
        got_outer.append([
            remote(own, full.at[k, outer_at(n_out - d), inner, core], zgs.at[k, d - 1], zgr.at[k, d - 1],
                   device(outer_at(d), inner, core))
            for d in range(1, n_out)
        ])
        line = full.at[k, :, inner, core]
        gather_inner.append([
            remote(line, line, xgs.at[k, d - 1], xgr.at[k, d - 1], device(outer, inner_at(d), core))
            for d in range(1, n_in)
        ])
        got_inner.append([
            remote(line, full.at[k, :, inner_at(n_in - d), core], xgs.at[k, d - 1], xgr.at[k, d - 1],
                   device(outer, inner_at(d), core))
            for d in range(1, n_in)
        ])
        half = full.at[k, :, :, core]
        gather_core.append(remote(half, half, cgs.at[k], cgr.at[k], sibling))
        got_core.append(remote(half, full.at[k, :, :, 1 - core], cgs.at[k], cgr.at[k], sibling))
        to_next.append(remote(after.at[k], resid.at[k], ys.at[k], yr.at[k], (lax.rem(feat + 1, n_feat), me)))

    def partial_of(k, scaled):
        value = jnp.dot(xt[...], scaled, preferred_element_type=jnp.float32)
        part[k] = value.reshape(part.shape[1:])
        to_core[k].start()

    def stage_partial(k):
        @pl.when(feat > 0)
        def _():
            to_next[k].wait_recv()
            partial_of(k, (row_weight[...] * resid[k]).astype(jnp.bfloat16))

    def stage_inner(k):
        to_core[k].wait_recv()
        sum1[k] = part[k, :, :, core] + core_in[k]
        for copy in to_inner[k]:
            copy.start()

    def stage_outer(k):
        total = sum1[k, :, inner]
        for d, copy in enumerate(to_inner[k]):
            copy.wait_recv()
            total = total + inner_in[k, d]
        sum2[k] = total
        for copy in to_outer[k]:
            copy.start()

    def stage_own(k):
        total = sum2[k, outer]
        for d, copy in enumerate(to_outer[k]):
            copy.wait_recv()
            total = total + outer_in[k, d]
        full[k, outer, inner, core] = total * scale[0:1, k * CHUNK:(k + 1) * CHUNK]
        for copy in gather_outer[k]:
            copy.start()

    def stage_gather_inner(k):
        for copy in got_outer[k]:
            copy.wait_recv()
        for copy in gather_inner[k]:
            copy.start()

    def stage_gather_core(k):
        for copy in got_inner[k]:
            copy.wait_recv()
        gather_core[k].start()

    def stage_update(k):
        got_core[k].wait_recv()
        high, low = split(full[k].reshape(width, CHUNK))
        mh = m_high[...]
        value = jnp.dot(mh, high, preferred_element_type=jnp.float32)
        value = value + jnp.dot(mh, low, preferred_element_type=jnp.float32)
        value = value + jnp.dot(m_low[...], high, preferred_element_type=jnp.float32)
        updated = resid[k] - value[0:rows]
        after[k] = updated

        @pl.when(feat < n_feat - 1)
        def _():
            to_next[k].start()

        out_ref[0, :, k * CHUNK:(k + 1) * CHUNK] = updated
        w_ref[:, k * CHUNK:(k + 1) * CHUNK] = value[rows:rows + share]

    @pl.when(feat == 0)
    def _():
        for k in range(chunks):
            partial_of(k, resid[k].astype(jnp.bfloat16))

    count_core()

    @pl.when(feat > 0)
    def _():
        count_inner()
        weights_of_rows()
        products()

    stages = [
        stage_partial, stage_inner, stage_outer, stage_own, stage_gather_inner, stage_gather_core, stage_update,
    ]
    for s, k in order:
        if (s, k) == (3, 0):
            @pl.when(feat == 0)
            def _():
                weights_of_classes()
        stages[s](k)
        if (s, k) == (1, 0):
            @pl.when(feat == 0)
            def _():
                count_inner()
        if (s, k) == (2, 0):
            @pl.when(feat == 0)
            def _():
                products()

    n_core.wait_send()
    for copy in n_inner + n_outer:
        copy.wait_send()
    for k in range(chunks):
        for copy in [to_core[k], gather_core[k]] + to_inner[k] + to_outer[k] + gather_outer[k] + gather_inner[k]:
            copy.wait_send()

    @pl.when(feat < n_feat - 1)
    def _():
        for k in range(chunks):
            to_next[k].wait_send()


def solution(mesh):
    n_feat = mesh.shape["feat"]
    n_rows = mesh.shape["rows"]
    n_out = math.gcd(4, n_rows // CORES)
    n_in = n_rows // CORES // n_out
    chunks = C // CHUNK
    order = sorted(
        ((s, k) for s in range(7) for k in range(chunks)), key=lambda at: (at[1] + 1.5 * at[0], -at[0])
    )

    def local(features, labels, inv_gram):
        rows, width = features.shape
        share = width // n_rows
        f32, bf16 = jnp.float32, jnp.bfloat16
        dma = pltpu.SemaphoreType.DMA
        vmem = pltpu.VMEM
        near, far = max(n_in - 1, 1), max(n_out - 1, 1)
        piece = (share, CHUNK)
        pair = lambda *shape: [dma(shape), dma(shape)]
        flops = 2 * rows * width * (2 * width + 4 * C)
        return pl.pallas_call(
            functools.partial(kernel, (n_feat, n_out, n_in), float(rows * n_rows), order),
            out_shape=(
                jax.ShapeDtypeStruct((share, C), f32),
                jax.ShapeDtypeStruct((1, rows, C), f32),
            ),
            in_specs=[
                pl.BlockSpec(memory_space=pltpu.VMEM),
                pl.BlockSpec(memory_space=pltpu.VMEM),
                pl.BlockSpec(memory_space=pl.ANY),
            ],
            out_specs=(pl.BlockSpec(memory_space=pltpu.VMEM), pl.BlockSpec(memory_space=pltpu.VMEM)),
            scratch_shapes=[
                vmem((width, width), f32),
                vmem((width, rows), bf16),
                vmem((rows + share, width), bf16),
                vmem((rows + share, width), bf16),
                vmem((chunks, n_out, n_in, CORES) + piece, f32),
                vmem((chunks, n_out, n_in) + piece, f32),
                vmem((chunks, n_out, n_in) + piece, f32),
                vmem((chunks, near, n_out) + piece, f32),
                vmem((chunks, n_out) + piece, f32),
                vmem((chunks, far) + piece, f32),
                vmem((chunks, n_out, n_in, CORES) + piece, f32),
                vmem((chunks, rows, CHUNK), f32),
                vmem((chunks, rows, CHUNK), f32),
                vmem((rows, 1), f32),
                vmem((8, C), f32),
                vmem((3, 8, C), f32),
                vmem((8, C), f32),
                vmem((near, 8, C), f32),
                vmem((far, 8, C), f32),
                dma,
                *pair(chunks), *pair(chunks, near), *pair(chunks, far), *pair(chunks, far), *pair(chunks, near),
                *pair(chunks), *pair(chunks), dma, dma, *pair(near), *pair(far),
            ],
            compiler_params=pltpu.CompilerParams(
                collective_id=0, has_side_effects=True, vmem_limit_bytes=60 * 1024 * 1024
            ),
            cost_estimate=pl.CostEstimate(flops=flops, bytes_accessed=6 << 20, transcendentals=0),
        )(features, labels[:, None], inv_gram[0])

    in_specs = (P("rows", "feat"), P("rows"), P("feat", None, None))
    out_specs = (P(("feat", "rows"), None), P("feat", "rows", None))
    return jax.shard_map(local, mesh=mesh, in_specs=in_specs, out_specs=out_specs, check_vma=False)
```

```python
import functools
import math

import jax
import jax.numpy as jnp
from jax import lax
from jax.experimental import pallas as pl
from jax.experimental.pallas import tpu as pltpu
from jax.sharding import PartitionSpec as P

C = 640
CHUNK = 128
CORES = 2
MESH = pl.DeviceIdType.MESH


def split(value):
    high = value.astype(jnp.bfloat16)
    return high, (value - high.astype(jnp.float32)).astype(jnp.bfloat16)


def kernel(
    groups, total_rows, order,
    x_ref, labels_ref, inv_ref, w_ref, out_ref,
    inv, xt, m_high, m_low, part, core_in, sum1, inner_in, sum2, outer_in, full, resid, after,
    row_weight, scale, cnt, cnt_core, cnt_inner, cnt_outer,
    inv_sem, cs, cr, xs, xr, zs, zr, zgs, zgr, xgs, xgr, cgs, cgr, ys, yr, ncs, ncr, nxs, nxr, nzs, nzr,
):
    n_feat, n_out, n_in = groups
    feat = lax.axis_index("feat")
    me = lax.axis_index("rows")
    core = lax.rem(me, CORES)
    inner = lax.rem(me // CORES, n_in)
    outer = me // (CORES * n_in)
    rows, width = x_ref.shape
    share = part.shape[-2]
    chunks = part.shape[0]

    def device(o, i, c):
        return (feat, (o * n_in + i) * CORES + c)

    sibling = device(outer, inner, 1 - core)

    def inner_at(d):
        return lax.rem(inner + d, n_in)

    def outer_at(d):
        return lax.rem(outer + d, n_out)

    def remote(src, dst, send, recv, where):
        return pltpu.make_async_remote_copy(
            src_ref=src, dst_ref=dst, send_sem=send, recv_sem=recv, device_id=where, device_id_type=MESH
        )

    inv_copy = pltpu.make_async_copy(inv_ref, inv, inv_sem)
    inv_copy.start()

    barrier = pltpu.get_barrier_semaphore()
    peers = [sibling]
    peers += [device(outer, inner_at(d), core) for d in range(1, n_in)]
    peers += [device(outer_at(d), inner, core) for d in range(1, n_out)]
    for peer in peers:
        pl.semaphore_signal(barrier, inc=1, device_id=peer, device_id_type=MESH)

    @pl.when(feat < n_feat - 1)
    def _():
        pl.semaphore_signal(barrier, inc=1, device_id=(feat + 1, me), device_id_type=MESH)

    @pl.when(feat > 0)
    def _():
        pl.semaphore_signal(barrier, inc=1, device_id=(feat - 1, me), device_id_type=MESH)

    labels = labels_ref[...]
    onehot = (labels == lax.broadcasted_iota(jnp.int32, (rows, C), 1)).astype(jnp.float32)
    cnt[0] = jnp.broadcast_to(jnp.sum(onehot, axis=0, keepdims=True), (8, C))

    @pl.when(feat == 0)
    def _():
        for k in range(chunks):
            resid[k] = onehot[:, k * CHUNK:(k + 1) * CHUNK]

    xt[...] = x_ref[...].T

    beside = (feat < n_feat - 1).astype(jnp.int32) + (feat > 0).astype(jnp.int32)
    pl.semaphore_wait(barrier, len(peers) + beside)

    n_core = remote(cnt.at[0], cnt_core, ncs, ncr, sibling)
    n_core.start()
    n_inner = [
        remote(cnt.at[1], cnt_inner.at[d - 1], nxs.at[d - 1], nxr.at[d - 1], device(outer, inner_at(d), core))
        for d in range(1, n_in)
    ]
    n_outer = [
        remote(cnt.at[2], cnt_outer.at[d - 1], nzs.at[d - 1], nzr.at[d - 1], device(outer_at(d), inner, core))
        for d in range(1, n_out)
    ]

    def count_core():
        n_core.wait_recv()
        cnt[1] = cnt[0] + cnt_core[...]
        for copy in n_inner:
            copy.start()

    def count_inner():
        total = cnt[1]
        for d, copy in enumerate(n_inner):
            copy.wait_recv()
            total = total + cnt_inner[d]
        cnt[2] = total
        for copy in n_outer:
            copy.start()

    def count_outer():
        total = cnt[2]
        for d, copy in enumerate(n_outer):
            copy.wait_recv()
            total = total + cnt_outer[d]
        return total

    def weights_of_classes():
        counts = count_outer()
        by_class = jnp.where(counts > 0, total_rows / (C * jnp.maximum(counts, 1.0)), 0.0)
        scale[...] = by_class.astype(jnp.bfloat16).astype(jnp.float32)

    def weights_of_rows():
        counts = count_outer()
        hot = (labels_ref[...] == lax.broadcasted_iota(jnp.int32, (rows, C), 1)).astype(jnp.float32)
        count_row = jnp.sum(hot * counts[0:1], axis=1, keepdims=True)
        row_weight[...] = total_rows / (C * count_row)
        scale[...] = jnp.ones_like(scale)

    def products():
        inv_copy.wait()
        block = min(256, width)

        @pl.loop(0, width // block)
        def _(j):
            columns = pl.ds(pl.multiple_of(j * block, block), block)
            high, low = split(inv[:, columns])
            x = x_ref[...]
            m = jnp.dot(x, high, preferred_element_type=jnp.float32)
            m = m + jnp.dot(x, low, preferred_element_type=jnp.float32)
            mh, ml = split(m)
            m_high[0:rows, columns] = mh
            m_low[0:rows, columns] = ml

        oh, ol = split(inv[pl.ds(pl.multiple_of(me * share, share), share), :])
        m_high[rows:rows + share, :] = oh
        m_low[rows:rows + share, :] = ol

    to_core, to_inner, to_outer, gather_outer, gather_inner, gather_core, to_next = [], [], [], [], [], [], []
    got_outer, got_inner, got_core = [], [], []
    for k in range(chunks):
        to_core.append(remote(part.at[k, :, :, 1 - core], core_in.at[k], cs.at[k], cr.at[k], sibling))
        to_inner.append([
            remote(sum1.at[k, :, inner_at(d)], inner_in.at[k, d - 1], xs.at[k, d - 1], xr.at[k, d - 1],
                   device(outer, inner_at(d), core))
            for d in range(1, n_in)
        ])
        to_outer.append([
            remote(sum2.at[k, outer_at(d)], outer_in.at[k, d - 1], zs.at[k, d - 1], zr.at[k, d - 1],
                   device(outer_at(d), inner, core))
            for d in range(1, n_out)
        ])
        own = full.at[k, outer, inner, core]
        gather_outer.append([
            remote(own, own, zgs.at[k, d - 1], zgr.at[k, d - 1], device(outer_at(d), inner, core))
            for d in range(1, n_out)
        ])
        got_outer.append([
            remote(own, full.at[k, outer_at(n_out - d), inner, core], zgs.at[k, d - 1], zgr.at[k, d - 1],
                   device(outer_at(d), inner, core))
            for d in range(1, n_out)
        ])
        line = full.at[k, :, inner, core]
        gather_inner.append([
            remote(line, line, xgs.at[k, d - 1], xgr.at[k, d - 1], device(outer, inner_at(d), core))
            for d in range(1, n_in)
        ])
        got_inner.append([
            remote(line, full.at[k, :, inner_at(n_in - d), core], xgs.at[k, d - 1], xgr.at[k, d - 1],
                   device(outer, inner_at(d), core))
            for d in range(1, n_in)
        ])
        half = full.at[k, :, :, core]
        gather_core.append(remote(half, half, cgs.at[k], cgr.at[k], sibling))
        got_core.append(remote(half, full.at[k, :, :, 1 - core], cgs.at[k], cgr.at[k], sibling))
        to_next.append(remote(after.at[k], resid.at[k], ys.at[k], yr.at[k], (lax.rem(feat + 1, n_feat), me)))

    def partial_of(k, scaled):
        value = jnp.dot(xt[...], scaled, preferred_element_type=jnp.float32)
        part[k] = value.reshape(part.shape[1:])
        to_core[k].start()

    def stage_partial(k):
        @pl.when(feat > 0)
        def _():
            to_next[k].wait_recv()
            partial_of(k, (row_weight[...] * resid[k]).astype(jnp.bfloat16))

    def stage_inner(k):
        to_core[k].wait_recv()
        sum1[k] = part[k, :, :, core] + core_in[k]
        for copy in to_inner[k]:
            copy.start()

    def stage_outer(k):
        total = sum1[k, :, inner]
        for d, copy in enumerate(to_inner[k]):
            copy.wait_recv()
            total = total + inner_in[k, d]
        sum2[k] = total
        for copy in to_outer[k]:
            copy.start()

    def stage_own(k):
        total = sum2[k, outer]
        for d, copy in enumerate(to_outer[k]):
            copy.wait_recv()
            total = total + outer_in[k, d]
        full[k, outer, inner, core] = total * scale[0:1, k * CHUNK:(k + 1) * CHUNK]
        for copy in gather_outer[k]:
            copy.start()

    def stage_gather_inner(k):
        for copy in got_outer[k]:
            copy.wait_recv()
        for copy in gather_inner[k]:
            copy.start()

    def stage_gather_core(k):
        for copy in got_inner[k]:
            copy.wait_recv()
        gather_core[k].start()

    def stage_update(k):
        got_core[k].wait_recv()
        high, low = split(full[k].reshape(width, CHUNK))
        mh = m_high[...]
        value = jnp.dot(mh, high, preferred_element_type=jnp.float32)
        value = value + jnp.dot(mh, low, preferred_element_type=jnp.float32)
        value = value + jnp.dot(m_low[...], high, preferred_element_type=jnp.float32)
        updated = resid[k] - value[0:rows]
        after[k] = updated

        @pl.when(feat < n_feat - 1)
        def _():
            to_next[k].start()

        out_ref[0, :, k * CHUNK:(k + 1) * CHUNK] = updated
        w_ref[:, k * CHUNK:(k + 1) * CHUNK] = value[rows:rows + share]

    @pl.when(feat == 0)
    def _():
        for k in range(chunks):
            partial_of(k, resid[k].astype(jnp.bfloat16))

    count_core()

    @pl.when(feat > 0)
    def _():
        count_inner()
        weights_of_rows()
        products()

    stages = [
        stage_partial, stage_inner, stage_outer, stage_own, stage_gather_inner, stage_gather_core, stage_update,
    ]
    for s, k in order:
        if (s, k) == (3, 0):
            @pl.when(feat == 0)
            def _():
                weights_of_classes()
        stages[s](k)
        if (s, k) == (1, 0):
            @pl.when(feat == 0)
            def _():
                count_inner()
        if (s, k) == (2, 0):
            @pl.when(feat == 0)
            def _():
                products()

    n_core.wait_send()
    for copy in n_inner + n_outer:
        copy.wait_send()
    for k in range(chunks):
        for copy in [to_core[k], gather_core[k]] + to_inner[k] + to_outer[k] + gather_outer[k] + gather_inner[k]:
            copy.wait_send()

    @pl.when(feat < n_feat - 1)
    def _():
        for k in range(chunks):
            to_next[k].wait_send()


def solution(mesh):
    n_feat = mesh.shape["feat"]
    n_rows = mesh.shape["rows"]
    n_out = math.gcd(4, n_rows // CORES)
    n_in = n_rows // CORES // n_out
    chunks = C // CHUNK
    order = sorted(
        ((s, k) for s in range(7) for k in range(chunks)), key=lambda at: (1.0 * at[1] + at[0], -at[0])
    )

    def local(features, labels, inv_gram):
        rows, width = features.shape
        share = width // n_rows
        f32, bf16 = jnp.float32, jnp.bfloat16
        dma = pltpu.SemaphoreType.DMA
        vmem = pltpu.VMEM
        near, far = max(n_in - 1, 1), max(n_out - 1, 1)
        piece = (share, CHUNK)
        pair = lambda *shape: [dma(shape), dma(shape)]
        flops = 2 * rows * width * (2 * width + 4 * C)
        return pl.pallas_call(
            functools.partial(kernel, (n_feat, n_out, n_in), float(rows * n_rows), order),
            out_shape=(
                jax.ShapeDtypeStruct((share, C), f32),
                jax.ShapeDtypeStruct((1, rows, C), f32),
            ),
            in_specs=[
                pl.BlockSpec(memory_space=pltpu.VMEM),
                pl.BlockSpec(memory_space=pltpu.VMEM),
                pl.BlockSpec(memory_space=pl.ANY),
            ],
            out_specs=(pl.BlockSpec(memory_space=pltpu.VMEM), pl.BlockSpec(memory_space=pltpu.VMEM)),
            scratch_shapes=[
                vmem((width, width), f32),
                vmem((width, rows), bf16),
                vmem((rows + share, width), bf16),
                vmem((rows + share, width), bf16),
                vmem((chunks, n_out, n_in, CORES) + piece, f32),
                vmem((chunks, n_out, n_in) + piece, f32),
                vmem((chunks, n_out, n_in) + piece, f32),
                vmem((chunks, near, n_out) + piece, f32),
                vmem((chunks, n_out) + piece, f32),
                vmem((chunks, far) + piece, f32),
                vmem((chunks, n_out, n_in, CORES) + piece, f32),
                vmem((chunks, rows, CHUNK), f32),
                vmem((chunks, rows, CHUNK), f32),
                vmem((rows, 1), f32),
                vmem((8, C), f32),
                vmem((3, 8, C), f32),
                vmem((8, C), f32),
                vmem((near, 8, C), f32),
                vmem((far, 8, C), f32),
                dma,
                *pair(chunks), *pair(chunks, near), *pair(chunks, far), *pair(chunks, far), *pair(chunks, near),
                *pair(chunks), *pair(chunks), dma, dma, *pair(near), *pair(far),
            ],
            compiler_params=pltpu.CompilerParams(
                collective_id=0, has_side_effects=True, vmem_limit_bytes=60 * 1024 * 1024
            ),
            cost_estimate=pl.CostEstimate(flops=flops, bytes_accessed=6 << 20, transcendentals=0),
        )(features, labels[:, None], inv_gram[0])

    in_specs = (P("rows", "feat"), P("rows"), P("feat", None, None))
    out_specs = (P(("feat", "rows"), None), P("feat", "rows", None))
    return jax.shard_map(local, mesh=mesh, in_specs=in_specs, out_specs=out_specs, check_vma=False)
```

```python
import functools
import math

import jax
import jax.numpy as jnp
from jax import lax
from jax.experimental import pallas as pl
from jax.experimental.pallas import tpu as pltpu
from jax.sharding import PartitionSpec as P

C = 640
CHUNK = 128
CORES = 2
MESH = pl.DeviceIdType.MESH


def split(value):
    high = value.astype(jnp.bfloat16)
    return high, (value - high.astype(jnp.float32)).astype(jnp.bfloat16)


def kernel(
    groups, total_rows, order,
    x_ref, labels_ref, inv_ref, w_ref, out_ref,
    inv, xt, m_high, m_low, part, core_in, sum1, inner_in, sum2, outer_in, full, resid, after,
    row_weight, scale, cnt, cnt_core, cnt_inner, cnt_outer,
    inv_sem, cs, cr, xs, xr, zs, zr, zgs, zgr, xgs, xgr, cgs, cgr, ys, yr, ncs, ncr, nxs, nxr, nzs, nzr,
):
    n_feat, n_out, n_in = groups
    feat = lax.axis_index("feat")
    me = lax.axis_index("rows")
    core = lax.rem(me, CORES)
    inner = lax.rem(me // CORES, n_in)
    outer = me // (CORES * n_in)
    rows, width = x_ref.shape
    share = part.shape[-2]
    chunks = part.shape[0]

    def device(o, i, c):
        return (feat, (o * n_in + i) * CORES + c)

    sibling = device(outer, inner, 1 - core)

    def inner_at(d):
        return lax.rem(inner + d, n_in)

    def outer_at(d):
        return lax.rem(outer + d, n_out)

    def remote(src, dst, send, recv, where):
        return pltpu.make_async_remote_copy(
            src_ref=src, dst_ref=dst, send_sem=send, recv_sem=recv, device_id=where, device_id_type=MESH
        )

    inv_copy = pltpu.make_async_copy(inv_ref, inv, inv_sem)
    inv_copy.start()

    barrier = pltpu.get_barrier_semaphore()
    peers = [sibling]
    peers += [device(outer, inner_at(d), core) for d in range(1, n_in)]
    peers += [device(outer_at(d), inner, core) for d in range(1, n_out)]
    for peer in peers:
        pl.semaphore_signal(barrier, inc=1, device_id=peer, device_id_type=MESH)

    @pl.when(feat < n_feat - 1)
    def _():
        pl.semaphore_signal(barrier, inc=1, device_id=(feat + 1, me), device_id_type=MESH)

    @pl.when(feat > 0)
    def _():
        pl.semaphore_signal(barrier, inc=1, device_id=(feat - 1, me), device_id_type=MESH)

    labels = jnp.broadcast_to(labels_ref[...], (CHUNK, rows)).T[:, 0:1]
    onehot = (labels == lax.broadcasted_iota(jnp.int32, (rows, C), 1)).astype(jnp.float32)
    cnt[0] = jnp.broadcast_to(jnp.sum(onehot, axis=0, keepdims=True), (8, C))

    @pl.when(feat == 0)
    def _():
        for k in range(chunks):
            resid[k] = onehot[:, k * CHUNK:(k + 1) * CHUNK]

    xt[...] = x_ref[...].T

    beside = (feat < n_feat - 1).astype(jnp.int32) + (feat > 0).astype(jnp.int32)
    pl.semaphore_wait(barrier, len(peers) + beside)

    n_core = remote(cnt.at[0], cnt_core, ncs, ncr, sibling)
    n_core.start()
    n_inner = [
        remote(cnt.at[1], cnt_inner.at[d - 1], nxs.at[d - 1], nxr.at[d - 1], device(outer, inner_at(d), core))
        for d in range(1, n_in)
    ]
    n_outer = [
        remote(cnt.at[2], cnt_outer.at[d - 1], nzs.at[d - 1], nzr.at[d - 1], device(outer_at(d), inner, core))
        for d in range(1, n_out)
    ]

    def count_core():
        n_core.wait_recv()
        cnt[1] = cnt[0] + cnt_core[...]
        for copy in n_inner:
            copy.start()

    def count_inner():
        total = cnt[1]
        for d, copy in enumerate(n_inner):
            copy.wait_recv()
            total = total + cnt_inner[d]
        cnt[2] = total
        for copy in n_outer:
            copy.start()

    def count_outer():
        total = cnt[2]
        for d, copy in enumerate(n_outer):
            copy.wait_recv()
            total = total + cnt_outer[d]
        return total

    def weights_of_classes():
        counts = count_outer()
        by_class = jnp.where(counts > 0, total_rows / (C * jnp.maximum(counts, 1.0)), 0.0)
        scale[...] = by_class.astype(jnp.bfloat16).astype(jnp.float32)

    def weights_of_rows():
        counts = count_outer()
        hot = (labels == lax.broadcasted_iota(jnp.int32, (rows, C), 1)).astype(jnp.float32)
        count_row = jnp.sum(hot * counts[0:1], axis=1, keepdims=True)
        row_weight[...] = total_rows / (C * count_row)
        scale[...] = jnp.ones_like(scale)

    def products():
        inv_copy.wait()
        block = min(256, width)

        @pl.loop(0, width // block)
        def _(j):
            columns = pl.ds(pl.multiple_of(j * block, block), block)
            high, low = split(inv[:, columns])
            x = x_ref[...]
            m = jnp.dot(x, high, preferred_element_type=jnp.float32)
            m = m + jnp.dot(x, low, preferred_element_type=jnp.float32)
            mh, ml = split(m)
            m_high[0:rows, columns] = mh
            m_low[0:rows, columns] = ml

        oh, ol = split(inv[pl.ds(pl.multiple_of(me * share, share), share), :])
        m_high[rows:rows + share, :] = oh
        m_low[rows:rows + share, :] = ol

    to_core, to_inner, to_outer, gather_outer, gather_inner, gather_core, to_next = [], [], [], [], [], [], []
    got_outer, got_inner, got_core = [], [], []
    for k in range(chunks):
        to_core.append(remote(part.at[k, :, :, 1 - core], core_in.at[k], cs.at[k], cr.at[k], sibling))
        to_inner.append([
            remote(sum1.at[k, :, inner_at(d)], inner_in.at[k, d - 1], xs.at[k, d - 1], xr.at[k, d - 1],
                   device(outer, inner_at(d), core))
            for d in range(1, n_in)
        ])
        to_outer.append([
            remote(sum2.at[k, outer_at(d)], outer_in.at[k, d - 1], zs.at[k, d - 1], zr.at[k, d - 1],
                   device(outer_at(d), inner, core))
            for d in range(1, n_out)
        ])
        own = full.at[k, outer, inner, core]
        gather_outer.append([
            remote(own, own, zgs.at[k, d - 1], zgr.at[k, d - 1], device(outer_at(d), inner, core))
            for d in range(1, n_out)
        ])
        got_outer.append([
            remote(own, full.at[k, outer_at(n_out - d), inner, core], zgs.at[k, d - 1], zgr.at[k, d - 1],
                   device(outer_at(d), inner, core))
            for d in range(1, n_out)
        ])
        line = full.at[k, :, inner, core]
        gather_inner.append([
            remote(line, line, xgs.at[k, d - 1], xgr.at[k, d - 1], device(outer, inner_at(d), core))
            for d in range(1, n_in)
        ])
        got_inner.append([
            remote(line, full.at[k, :, inner_at(n_in - d), core], xgs.at[k, d - 1], xgr.at[k, d - 1],
                   device(outer, inner_at(d), core))
            for d in range(1, n_in)
        ])
        half = full.at[k, :, :, core]
        gather_core.append(remote(half, half, cgs.at[k], cgr.at[k], sibling))
        got_core.append(remote(half, full.at[k, :, :, 1 - core], cgs.at[k], cgr.at[k], sibling))
        to_next.append(remote(after.at[k], resid.at[k], ys.at[k], yr.at[k], (lax.rem(feat + 1, n_feat), me)))

    def partial_of(k, scaled):
        value = jnp.dot(xt[...], scaled, preferred_element_type=jnp.float32)
        part[k] = value.reshape(part.shape[1:])
        to_core[k].start()

    def stage_partial(k):
        @pl.when(feat > 0)
        def _():
            to_next[k].wait_recv()
            partial_of(k, (row_weight[...] * resid[k]).astype(jnp.bfloat16))

    def stage_inner(k):
        to_core[k].wait_recv()
        sum1[k] = part[k, :, :, core] + core_in[k]
        for copy in to_inner[k]:
            copy.start()

    def stage_outer(k):
        total = sum1[k, :, inner]
        for d, copy in enumerate(to_inner[k]):
            copy.wait_recv()
            total = total + inner_in[k, d]
        sum2[k] = total
        for copy in to_outer[k]:
            copy.start()

    def stage_own(k):
        total = sum2[k, outer]
        for d, copy in enumerate(to_outer[k]):
            copy.wait_recv()
            total = total + outer_in[k, d]
        full[k, outer, inner, core] = total * scale[0:1, k * CHUNK:(k + 1) * CHUNK]
        for copy in gather_outer[k]:
            copy.start()

    def stage_gather_inner(k):
        for copy in got_outer[k]:
            copy.wait_recv()
        for copy in gather_inner[k]:
            copy.start()

    def stage_gather_core(k):
        for copy in got_inner[k]:
            copy.wait_recv()
        gather_core[k].start()

    def stage_update(k):
        got_core[k].wait_recv()
        high, low = split(full[k].reshape(width, CHUNK))
        mh = m_high[...]
        value = jnp.dot(mh, high, preferred_element_type=jnp.float32)
        value = value + jnp.dot(mh, low, preferred_element_type=jnp.float32)
        value = value + jnp.dot(m_low[...], high, preferred_element_type=jnp.float32)
        updated = resid[k] - value[0:rows]
        after[k] = updated

        @pl.when(feat < n_feat - 1)
        def _():
            to_next[k].start()

        out_ref[0, :, k * CHUNK:(k + 1) * CHUNK] = updated
        w_ref[:, k * CHUNK:(k + 1) * CHUNK] = value[rows:rows + share]

    @pl.when(feat == 0)
    def _():
        for k in range(chunks):
            partial_of(k, resid[k].astype(jnp.bfloat16))

    count_core()

    @pl.when(feat > 0)
    def _():
        count_inner()
        weights_of_rows()
        products()

    stages = [
        stage_partial, stage_inner, stage_outer, stage_own, stage_gather_inner, stage_gather_core, stage_update,
    ]
    for s, k in order:
        if (s, k) == (3, 0):
            @pl.when(feat == 0)
            def _():
                weights_of_classes()
        stages[s](k)
        if (s, k) == (1, 0):
            @pl.when(feat == 0)
            def _():
                count_inner()
        if (s, k) == (2, 0):
            @pl.when(feat == 0)
            def _():
                products()

    n_core.wait_send()
    for copy in n_inner + n_outer:
        copy.wait_send()
    for k in range(chunks):
        for copy in [to_core[k], gather_core[k]] + to_inner[k] + to_outer[k] + gather_outer[k] + gather_inner[k]:
            copy.wait_send()

    @pl.when(feat < n_feat - 1)
    def _():
        for k in range(chunks):
            to_next[k].wait_send()


def solution(mesh):
    n_feat = mesh.shape["feat"]
    n_rows = mesh.shape["rows"]
    n_out = math.gcd(4, n_rows // CORES)
    n_in = n_rows // CORES // n_out
    chunks = C // CHUNK
    order = sorted(
        ((s, k) for s in range(7) for k in range(chunks)), key=lambda at: (1.0 * at[1] + at[0], -at[0])
    )

    def local(features, labels, inv_gram):
        rows, width = features.shape
        share = width // n_rows
        f32, bf16 = jnp.float32, jnp.bfloat16
        dma = pltpu.SemaphoreType.DMA
        vmem = pltpu.VMEM
        near, far = max(n_in - 1, 1), max(n_out - 1, 1)
        piece = (share, CHUNK)
        pair = lambda *shape: [dma(shape), dma(shape)]
        flops = 2 * rows * width * (2 * width + 4 * C)
        return pl.pallas_call(
            functools.partial(kernel, (n_feat, n_out, n_in), float(rows * n_rows), order),
            out_shape=(
                jax.ShapeDtypeStruct((share, C), f32),
                jax.ShapeDtypeStruct((1, rows, C), f32),
            ),
            in_specs=[
                pl.BlockSpec(memory_space=pltpu.VMEM),
                pl.BlockSpec(memory_space=pltpu.VMEM),
                pl.BlockSpec(memory_space=pl.ANY),
            ],
            out_specs=(pl.BlockSpec(memory_space=pltpu.VMEM), pl.BlockSpec(memory_space=pltpu.VMEM)),
            scratch_shapes=[
                vmem((width, width), f32),
                vmem((width, rows), bf16),
                vmem((rows + share, width), bf16),
                vmem((rows + share, width), bf16),
                vmem((chunks, n_out, n_in, CORES) + piece, f32),
                vmem((chunks, n_out, n_in) + piece, f32),
                vmem((chunks, n_out, n_in) + piece, f32),
                vmem((chunks, near, n_out) + piece, f32),
                vmem((chunks, n_out) + piece, f32),
                vmem((chunks, far) + piece, f32),
                vmem((chunks, n_out, n_in, CORES) + piece, f32),
                vmem((chunks, rows, CHUNK), f32),
                vmem((chunks, rows, CHUNK), f32),
                vmem((rows, 1), f32),
                vmem((8, C), f32),
                vmem((3, 8, C), f32),
                vmem((8, C), f32),
                vmem((near, 8, C), f32),
                vmem((far, 8, C), f32),
                dma,
                *pair(chunks), *pair(chunks, near), *pair(chunks, far), *pair(chunks, far), *pair(chunks, near),
                *pair(chunks), *pair(chunks), dma, dma, *pair(near), *pair(far),
            ],
            compiler_params=pltpu.CompilerParams(
                collective_id=0, has_side_effects=True, vmem_limit_bytes=60 * 1024 * 1024
            ),
            cost_estimate=pl.CostEstimate(flops=flops, bytes_accessed=6 << 20, transcendentals=0),
        )(features, labels[None, :], inv_gram[0])

    in_specs = (P("rows", "feat"), P("rows"), P("feat", None, None))
    out_specs = (P(("feat", "rows"), None), P("feat", "rows", None))
    return jax.shard_map(local, mesh=mesh, in_specs=in_specs, out_specs=out_specs, check_vma=False)
```
